32 devices in a mesh: dp: 4 (over y, x), expert: 8 (over z, core).
Axes of the slice: x: 2, y: 2, z: 4, core: 2. Of those that a mesh axis runs over, the one named last changes fastest.
Arguments:
- latents: bfloat16 [1024, 1024], P('expert'), may hold values from -6 to 6
- out_grad: bfloat16 [1024, 1024], P('expert'), may hold values from -6 to 6
- routes: int32 [1024, 8], P('expert'), may hold values from 0 to 63, all different within a row; in each aligned block of 128 rows (0 to 127, 128 to 255, ...) at most 32 rows name the same one
- route_weights: float32 [1024, 8], P('expert'), may hold values from 0.1 to 1
- gate_weight: bfloat16 [64, 1024, 768], P('expert', None, 'dp'), may hold values from -0.1875 to 0.1875
- up_weight: bfloat16 [64, 1024, 768], P('expert', None, 'dp'), may hold values from -0.1875 to 0.1875
- down_weight: bfloat16 [64, 1024, 768], P('expert', None, 'dp'), may hold values from -0.21875 to 0.21875
Outputs:
- mixed: bfloat16 [1024, 1024], P('expert')
- latent_grad: bfloat16 [1024, 1024], P('expert')
- weight_grad: float32 [1024, 8], P('expert')
The draws below stay inside these ranges and needn't reach their ends.
Inputs may be any that keep to these rules, and one draw needn't show every extreme that they name: `routes`: each row names 8 different experts. Among the rows of one index of expert no expert is named more than 32 times, and in every draw some index's rows name some expert exactly 32 times.
All inputs are finite; a program needn't handle non-finite values.
Results may differ from the reference program's by a relative error of at most 0.0064.
Values may be sent and summed in bfloat16 or wider, within the bound.
A program may use at most 128 MiB of HBM per device.

```python
import math
import jax
import jax.numpy as jnp
import numpy as np
from jax import lax

L = 1024
HID = 768
TOP = 8
TOK_DEV = 128
CAP = 32
EXPERTS = 64
TOKENS = 1024


def level_of(own_key, shape, split, smallest, high):
    factor_of = 1.0
    for axis_at, parts in split:
        draws = jax.random.uniform(jax.random.fold_in(jax.random.fold_in(own_key, 6), axis_at), (parts,), jnp.float32, smallest / len(split), high / len(split))
        factor_of = factor_of * jnp.repeat(jnp.exp(draws), shape[axis_at] // parts).reshape((-1,) + (1,) * (len(shape) - 1 - axis_at))
    return factor_of


def routed_block(stream_key, own, number, rows, number_of, top, most, skew):
    ranking = jax.random.permutation(stream_key, number_of)
    crowded, ordinary = load_shares(number_of, rows * top, most, skew, True), load_shares(number_of, rows * top, most, skew, False)
    places = jnp.arange(number_of)

    def named(sizes, turn):
        used = int((sizes > 0).sum())
        fixed = max(1, used // 4)
        moved = fixed + (places - fixed + turn * (used - fixed)) % max(1, number_of - fixed)
        return jnp.zeros((number_of,), jnp.int32).at[ranking[jnp.where(places < fixed, places, moved)]].set(jnp.asarray(sizes, jnp.int32))

    sizes = jnp.where(number % 4 == 0, named(crowded, number // 4), named(ordinary, number - number // 4 - 1))
    mixed = jax.random.permutation(jax.random.fold_in(own, 3), number_of)
    giver, receiver = mixed[0:number_of // 2 * 2:2], mixed[1:number_of // 2 * 2:2]
    room = jnp.minimum(sizes[giver] - 1, most - sizes[receiver]) // 2
    room = jnp.where((giver == ranking[0]) | (receiver == ranking[0]) | (sizes[receiver] == 0), 0, jnp.maximum(room, 0))
    moved = jax.random.randint(jax.random.fold_in(own, 4), (number_of // 2,), 0, 1 << 20) % (room + 1)
    sizes = sizes.at[giver].add(-moved).at[receiver].add(moved)
    items = jnp.searchsorted(jnp.cumsum(sizes), jnp.arange(rows * top), side="right").astype(jnp.int32)
    grid = items.reshape(top, rows).T
    grid = grid[jax.random.permutation(jax.random.fold_in(own, 1), rows)]
    turn = jax.random.randint(jax.random.fold_in(own, 2), (rows, 1), 0, top)
    return jnp.take_along_axis(grid, (jnp.arange(top)[None, :] + turn) % top, axis=1)


def load_shares(amount, total, most, skew, full):
    portions = [(1 << 20) // math.isqrt(grade ** skew) + 1 for grade in range(1, amount + 1)]
    largest = most if full else min(most, max(-(-total // amount), total * portions[0] // sum(portions)))
    least = 1 if total - largest >= amount - 1 else 0
    given, surplus = [largest] + [least] * (amount - 1), total - largest - least * (amount - 1)
    while surplus > 0:
        candidates = [i for i in range(1, amount) if given[i] < largest] or [i for i in range(1, amount) if given[i] < most]
        whole, left = sum([portions[i] for i in candidates]), surplus
        for i in candidates:
            more = min(most - given[i], max(1, left * portions[i] // whole), surplus)
            given[i] = given[i] + more
            surplus = surplus - more
    return np.array(given)


def scatter_about(own_key, dims, scale, limit, shards=(), held_as=jnp.bfloat16):
    loudness = level_of(own_key, dims, shards, -0.22, 0.18) if shards else 1.0
    array = jax.random.normal(own_key, dims, jnp.float32) * scale * loudness
    return jnp.minimum(jnp.maximum(array, -limit), limit).astype(held_as)


def setup_inputs(seed: int = 0) -> dict:
    key_of = jax.random.split(jax.random.key(seed), 8)
    latents = scatter_about(key_of[0], (TOKENS, L), 1.0, 6.0, ((0, 8),))
    out_grad = scatter_about(key_of[1], (TOKENS, L), 1.0, 6.0, ((0, 8),))
    routes_keys = jax.random.split(jax.random.fold_in(key_of[2], 1), TOKENS // TOK_DEV)
    routes_turns = jax.random.permutation(jax.random.fold_in(key_of[2], 3), TOKENS // TOK_DEV)
    routes = jax.vmap(lambda own, number: routed_block(jax.random.fold_in(key_of[2], 2), own, number, TOK_DEV, EXPERTS, TOP, CAP, 2))(routes_keys, routes_turns).reshape((TOKENS, TOP))
    route_weights = jnp.clip(jnp.exp(math.log(1.0) - 2.3025851 * jax.random.uniform(key_of[3], (TOKENS, TOP), jnp.float32) ** level_of(key_of[3], (TOKENS, TOP), ((0, 8),), -0.2, 0.2)), 0.1, 1.0)
    gate_weight = scatter_about(key_of[4], (EXPERTS, L, HID), L ** -0.5, 0.1875, ((0, 8), (2, 4)))
    up_weight = scatter_about(key_of[5], (EXPERTS, L, HID), L ** -0.5, 0.1875, ((0, 8), (2, 4)))
    down_weight = scatter_about(key_of[6], (EXPERTS, L, HID), HID ** -0.5, 0.21875, ((0, 8), (2, 4)))
    return dict(latents=latents, out_grad=out_grad, routes=routes, route_weights=route_weights, gate_weight=gate_weight, up_weight=up_weight, down_weight=down_weight)


def expert_slots(inputs, cotangent, gate_matrix, up_matrix, down_matrix):
    gate_act = jnp.dot(inputs, gate_matrix, preferred_element_type=jnp.float32)
    up_act = jnp.dot(inputs, up_matrix, preferred_element_type=jnp.float32)
    sigmoid_gate = jax.nn.sigmoid(gate_act)
    silu_gate = gate_act * sigmoid_gate
    hidden = (silu_gate * up_act).astype(jnp.bfloat16)
    output = jnp.dot(hidden, down_matrix.T, preferred_element_type=jnp.float32)
    grad_hidden = jnp.dot(cotangent, down_matrix, preferred_element_type=jnp.float32)
    slope = sigmoid_gate * (1.0 + gate_act * (1.0 - sigmoid_gate))
    grad_gate = (grad_hidden * up_act * slope).astype(jnp.bfloat16)
    grad_up = (grad_hidden * silu_gate).astype(jnp.bfloat16)
    grad_inputs = jnp.dot(grad_gate, gate_matrix.T, preferred_element_type=jnp.float32)
    grad_inputs = grad_inputs + jnp.dot(grad_up, up_matrix.T, preferred_element_type=jnp.float32)
    return output.astype(jnp.bfloat16), grad_inputs.astype(jnp.bfloat16)


def reference(latents, out_grad, routes, route_weights, gate_weight, up_weight, down_weight):
    blocks = TOKENS // TOK_DEV
    pair_count = TOKENS * TOP
    per_block = TOK_DEV * TOP
    chosen = routes.reshape(blocks, per_block).astype(jnp.int32)
    onehot = (chosen[:, :, None] == jnp.arange(EXPERTS, dtype=jnp.int32)[None, None, :]).astype(jnp.int32)
    before = jnp.cumsum(onehot, axis=1) - onehot
    position = jnp.sum(before * onehot, axis=2).astype(jnp.int32)
    block_ids = jnp.broadcast_to(jnp.arange(blocks, dtype=jnp.int32)[:, None], (blocks, per_block))
    pair_ids = jnp.arange(pair_count, dtype=jnp.int32).reshape(blocks, per_block)
    table = jnp.full((EXPERTS, blocks * CAP), pair_count, jnp.int32)
    table = table.at[chosen, block_ids * CAP + position].set(pair_ids)

    def one_expert(totals, expert):
        mixed_sum, grad_sum, weight_sum = totals
        entries = table[expert]
        valid = (entries < pair_count).astype(jnp.float32)
        clipped = jnp.minimum(entries, pair_count - 1)
        owners = clipped // TOP
        column = clipped % TOP
        weights = route_weights[owners, column] * valid
        upstream = out_grad[owners].astype(jnp.float32)
        cotangent = (weights[:, None] * upstream).astype(jnp.bfloat16)
        output, grad_inputs = expert_slots(latents[owners], cotangent, gate_weight[expert], up_weight[expert], down_weight[expert])
        output_wide = output.astype(jnp.float32)
        mixed_sum = mixed_sum.at[owners].add(weights[:, None] * output_wide)
        grad_sum = grad_sum.at[owners].add(valid[:, None] * grad_inputs.astype(jnp.float32))
        weight_sum = weight_sum.at[owners, column].add(valid * jnp.sum(upstream * output_wide, axis=1))
        return (mixed_sum, grad_sum, weight_sum), None

    start_state = (jnp.zeros((TOKENS, L), jnp.float32), jnp.zeros((TOKENS, L), jnp.float32), jnp.zeros((TOKENS, TOP), jnp.float32))
    totals, unused = lax.scan(one_expert, start_state, jnp.arange(EXPERTS, dtype=jnp.int32))
    return totals[0].astype(jnp.bfloat16), totals[1].astype(jnp.bfloat16), totals[2]
```

```python
import jax
import jax.numpy as jnp
from jax import lax
from jax.sharding import PartitionSpec as P


def local(latents, out_grad, routes, route_weights, gate_weight, up_weight, down_weight):
    features = latents.shape[1]
    local_experts = gate_weight.shape[0]
    groups = lax.axis_size("expert")
    experts = local_experts * groups
    me = lax.axis_index("expert")
    hot = routes[:, :, None] == jnp.arange(experts, dtype=jnp.int32)[None, None, :]
    table = jnp.sum(jnp.where(hot, route_weights[:, :, None], 0.0), axis=1)
    high = table.astype(jnp.bfloat16)
    low = (table - high.astype(jnp.float32)).astype(jnp.bfloat16)
    payload = jnp.concatenate([latents, out_grad, high, low], axis=1)
    got = lax.all_gather(payload, "expert", axis=0, tiled=True)
    tokens = got[:, :features]
    upstream = got[:, features : 2 * features]
    mine_high = lax.dynamic_slice_in_dim(got, 2 * features + me * local_experts, local_experts, 1)
    mine_low = lax.dynamic_slice_in_dim(
        got, 2 * features + experts + me * local_experts, local_experts, 1
    )
    weight = mine_high.astype(jnp.float32) + mine_low.astype(jnp.float32)
    weight = weight.T[:, :, None]
    gate_act = jnp.einsum("tl,elh->eth", tokens, gate_weight, preferred_element_type=jnp.float32)
    up_act = jnp.einsum("tl,elh->eth", tokens, up_weight, preferred_element_type=jnp.float32)
    back = jnp.einsum("tl,elh->eth", upstream, down_weight, preferred_element_type=jnp.float32)
    sig = jax.nn.sigmoid(gate_act)
    silu = gate_act * sig
    hidden = silu * up_act
    valid = (weight > 0).astype(jnp.float32)
    score = jnp.sum(hidden * back * valid, axis=2).T
    weighted = (hidden * weight).astype(jnp.bfloat16)
    back = back * weight
    slope = sig * (1.0 + gate_act * (1.0 - sig))
    grad_gate = (back * up_act * slope).astype(jnp.bfloat16)
    grad_up = (back * silu).astype(jnp.bfloat16)
    mixed = jnp.einsum("eth,elh->tl", weighted, down_weight, preferred_element_type=jnp.float32)
    grad = jnp.einsum("eth,elh->tl", grad_gate, gate_weight, preferred_element_type=jnp.float32)
    grad = grad + jnp.einsum("eth,elh->tl", grad_up, up_weight, preferred_element_type=jnp.float32)
    wide = jnp.zeros((got.shape[0], experts), jnp.float32)
    wide = lax.dynamic_update_slice_in_dim(wide, score, me * local_experts, 1)
    parts = jnp.concatenate([mixed, grad, wide], axis=1).astype(jnp.bfloat16)
    parts = parts.reshape(groups, latents.shape[0], parts.shape[1])
    moved = lax.all_to_all(parts, "expert", split_axis=0, concat_axis=0, tiled=True)
    summed = jnp.sum(moved.astype(jnp.float32), axis=0)
    total = lax.psum(summed, "dp")
    final = total[:, 2 * features :]
    weight_grad = jnp.sum(jnp.where(hot, final[:, None, :], 0.0), axis=2)
    return (
        total[:, :features].astype(jnp.bfloat16),
        total[:, features : 2 * features].astype(jnp.bfloat16),
        weight_grad,
    )


def solution(mesh):
    row = P("expert", None)
    cut = P("expert", None, "dp")
    return jax.shard_map(
        local,
        mesh=mesh,
        in_specs=(row, row, row, row, cut, cut, cut),
        out_specs=(row, row, row),
        check_vma=False,
    )
```

```python
import functools
import jax
import jax.numpy as jnp
from jax import lax
from jax.experimental import pallas as pl
from jax.experimental.pallas import tpu as pltpu
from jax.sharding import PartitionSpec as P

MESH = pl.DeviceIdType.MESH
WHOLE_BYTES = 8 << 20


def place(dp_count, z_count):
    d = lax.axis_index("dp")
    e = lax.axis_index("expert")
    z = e // 2
    c = e - 2 * z
    partner = (d, 2 * z + 1 - c)
    dp_to = [(lax.rem(d + k, dp_count), e) for k in range(dp_count)]
    dp_from = [lax.rem(d + dp_count - k, dp_count) for k in range(dp_count)]
    z_to = [lax.rem(z + j, z_count) for j in range(z_count)]
    z_from = [lax.rem(z + z_count - j, z_count) for j in range(z_count)]
    return d, z, c, partner, dp_to, dp_from, z_to, z_from


def greet(d, c, partner, dp_to, z_to):
    barrier = pltpu.get_barrier_semaphore()
    peers = [partner] + dp_to[1:] + [(d, 2 * zt + c) for zt in z_to[1:]]
    for peer in peers:
        pl.semaphore_signal(barrier, inc=1, device_id=peer, device_id_type=MESH)
    pl.semaphore_wait(barrier, len(peers))


def push(src, dst, send_sem, recv_sem, peer):
    return pltpu.make_async_remote_copy(
        src_ref=src,
        dst_ref=dst,
        send_sem=send_sem,
        recv_sem=recv_sem,
        device_id=peer,
        device_id_type=MESH,
    )


def gather_kernel(dp_count, z_count, own, out, local_sem, core_s, core_r, z_s, z_r, dp_s, dp_r):
    d, z, c, partner, dp_to, dp_from, z_to, z_from = place(dp_count, z_count)
    greet(d, c, partner, dp_to, z_to)
    sent = []
    for j in range(1, z_count):
        copy = push(own.at[d], out.at[z, c, d], z_s.at[j], z_r.at[j], (d, 2 * z_to[j] + c))
        copy.start()
        sent.append(copy)
    pair = push(own, out.at[z, c], core_s.at[0], core_r.at[0], partner)
    pair.start()
    sent.append(pair)
    keep = pltpu.make_async_copy(own, out.at[z, c], local_sem)
    keep.start()
    for j in range(1, z_count):
        zs = z_from[j]
        mine = out.at[zs, c, d]
        push(mine, mine, z_s.at[j], z_r.at[j], partner).wait_recv()
        for k in range(1, dp_count):
            copy = push(mine, mine, dp_s.at[j, k], dp_r.at[j, k], dp_to[k])
            copy.start()
            sent.append(copy)
    for j in range(1, z_count):
        zs = z_from[j]
        for k in range(1, dp_count):
            theirs = out.at[zs, c, dp_from[k]]
            push(theirs, theirs, dp_s.at[j, k], dp_r.at[j, k], partner).wait_recv()
        whole = out.at[zs, c]
        copy = push(whole, whole, core_s.at[j], core_r.at[j], partner)
        copy.start()
        sent.append(copy)
    keep.wait()
    for j in range(z_count):
        other = out.at[z_from[j], 1 - c]
        push(other, other, core_s.at[j], core_r.at[j], partner).wait_recv()
    for copy in sent:
        copy.wait_send()


def reduce_kernel(
    dp_count, z_count, parts, out, half, quarter, core_in, dp_in, z_in,
    core_s, core_r, dp_s, dp_r, z_s, z_r, end_s, end_r,
):
    d, z, c, partner, dp_to, dp_from, z_to, z_from = place(dp_count, z_count)
    greet(d, c, partner, dp_to, z_to)
    order = list(range(1, z_count)) + [0]
    sent = []
    for j in order:
        copy = push(
            parts.at[z_to[j], 1 - c], core_in.at[j], core_s.at[j], core_r.at[j], partner
        )
        copy.start()
        sent.append(copy)
    for j in order:
        push(core_in.at[j], core_in.at[j], core_s.at[j], core_r.at[j], partner).wait_recv()
        for k in list(range(1, dp_count)) + [0]:
            to = dp_to[k][0]
            half[j, k] = (
                parts[z_to[j], c, to].astype(jnp.float32) + core_in[j, to].astype(jnp.float32)
            ).astype(half.dtype)
            if k > 0:
                copy = push(
                    half.at[j, k], dp_in.at[j, k], dp_s.at[j, k], dp_r.at[j, k], dp_to[k]
                )
                copy.start()
                sent.append(copy)
    for j in order:
        total = half[j, 0].astype(jnp.float32)
        for k in range(1, dp_count):
            slot = dp_in.at[j, k]
            push(slot, slot, dp_s.at[j, k], dp_r.at[j, k], partner).wait_recv()
            total = total + dp_in[j, k].astype(jnp.float32)
        if j > 0:
            quarter[j] = total.astype(quarter.dtype)
            copy = push(
                quarter.at[j], z_in.at[j], z_s.at[j], z_r.at[j], (d, 2 * z_to[j] + c)
            )
            copy.start()
            sent.append(copy)
    for j in range(1, z_count):
        push(z_in.at[j], z_in.at[j], z_s.at[j], z_r.at[j], partner).wait_recv()
        total = total + z_in[j].astype(jnp.float32)
    out[d] = total.astype(out.dtype)
    for k in range(1, dp_count):
        copy = push(out.at[d], out.at[d], end_s.at[k], end_r.at[k], dp_to[k])
        copy.start()
        sent.append(copy)
    for k in range(1, dp_count):
        theirs = out.at[dp_from[k]]
        push(theirs, theirs, end_s.at[k], end_r.at[k], partner).wait_recv()
    for copy in sent:
        copy.wait_send()


def gather_rows(payload, dp_count, groups):
    rows, width = payload.shape
    z_count = groups // 2
    quarter = rows // dp_count
    dma = pltpu.SemaphoreType.DMA
    out = pl.pallas_call(
        functools.partial(gather_kernel, dp_count, z_count),
        out_shape=jax.ShapeDtypeStruct((z_count, 2, dp_count, quarter, width), payload.dtype),
        in_specs=[pl.BlockSpec(memory_space=pltpu.VMEM)],
        out_specs=pl.BlockSpec(memory_space=pltpu.VMEM),
        scratch_shapes=[dma]
        + [dma((z_count,))] * 4
        + [dma((z_count, dp_count))] * 2,
        compiler_params=pltpu.CompilerParams(
            collective_id=0, has_side_effects=True, vmem_limit_bytes=32 << 20
        ),
    )(payload.reshape(dp_count, quarter, width))
    return out.reshape(groups * rows, width)


def reduce_rows(parts, dp_count, groups):
    width = parts.shape[1]
    z_count = groups // 2
    quarter = parts.shape[0] // groups // dp_count
    dma = pltpu.SemaphoreType.DMA
    kind = parts.dtype
    out = pl.pallas_call(
        functools.partial(reduce_kernel, dp_count, z_count),
        out_shape=jax.ShapeDtypeStruct((dp_count, quarter, width), kind),
        in_specs=[pl.BlockSpec(memory_space=pltpu.VMEM)],
        out_specs=pl.BlockSpec(memory_space=pltpu.VMEM),
        scratch_shapes=[
            pltpu.VMEM((z_count, dp_count, quarter, width), kind),
            pltpu.VMEM((z_count, quarter, width), kind),
            pltpu.VMEM((z_count, dp_count, quarter, width), kind),
            pltpu.VMEM((z_count, dp_count, quarter, width), kind),
            pltpu.VMEM((z_count, quarter, width), kind),
        ]
        + [dma((z_count,))] * 2
        + [dma((z_count, dp_count))] * 2
        + [dma((z_count,))] * 2
        + [dma((dp_count,))] * 2,
        compiler_params=pltpu.CompilerParams(
            collective_id=1, has_side_effects=True, vmem_limit_bytes=48 << 20
        ),
    )(parts.reshape(z_count, 2, dp_count, quarter, width))
    return out.reshape(dp_count * quarter, width)


def local(latents, out_grad, routes, route_weights, gate_weight, up_weight, down_weight):
    features = latents.shape[1]
    local_experts = gate_weight.shape[0]
    groups = lax.axis_size("expert")
    experts = local_experts * groups
    me = lax.axis_index("expert")
    hot = routes[:, :, None] == jnp.arange(experts, dtype=jnp.int32)[None, None, :]
    table = jnp.sum(jnp.where(hot, route_weights[:, :, None], 0.0), axis=1)
    high = table.astype(jnp.bfloat16)
    low = (table - high.astype(jnp.float32)).astype(jnp.bfloat16)
    payload = jnp.concatenate([latents, out_grad, high, low], axis=1)
    dp_count = lax.axis_size("dp")
    rows = latents.shape[0]
    fits = rows % (16 * dp_count) == 0 and groups * payload.size * 2 <= WHOLE_BYTES
    if fits:
        got = gather_rows(payload, dp_count, groups)
    else:
        got = lax.all_gather(payload, "expert", axis=0, tiled=True)
    tokens = got[:, :features]
    upstream = got[:, features : 2 * features]
    mine_high = lax.dynamic_slice_in_dim(got, 2 * features + me * local_experts, local_experts, 1)
    mine_low = lax.dynamic_slice_in_dim(
        got, 2 * features + experts + me * local_experts, local_experts, 1
    )
    weight = mine_high.astype(jnp.float32) + mine_low.astype(jnp.float32)
    weight = weight.T[:, :, None]
    gate_act = jnp.einsum("tl,elh->eth", tokens, gate_weight, preferred_element_type=jnp.float32)
    up_act = jnp.einsum("tl,elh->eth", tokens, up_weight, preferred_element_type=jnp.float32)
    back = jnp.einsum("tl,elh->eth", upstream, down_weight, preferred_element_type=jnp.float32)
    sig = jax.nn.sigmoid(gate_act)
    silu = gate_act * sig
    hidden = silu * up_act
    valid = (weight > 0).astype(jnp.float32)
    score = jnp.sum(hidden * back * valid, axis=2).T
    weighted = (hidden * weight).astype(jnp.bfloat16)
    back = back * weight
    slope = sig * (1.0 + gate_act * (1.0 - sig))
    grad_gate = (back * up_act * slope).astype(jnp.bfloat16)
    grad_up = (back * silu).astype(jnp.bfloat16)
    mixed = jnp.einsum("eth,elh->tl", weighted, down_weight, preferred_element_type=jnp.float32)
    grad = jnp.einsum("eth,elh->tl", grad_gate, gate_weight, preferred_element_type=jnp.float32)
    grad = grad + jnp.einsum("eth,elh->tl", grad_up, up_weight, preferred_element_type=jnp.float32)
    wide = jnp.zeros((got.shape[0], 2 * experts), jnp.float32)
    wide = lax.dynamic_update_slice_in_dim(wide, score, me * local_experts, 1)
    parts = jnp.concatenate([mixed, grad, wide], axis=1).astype(jnp.bfloat16)
    if fits:
        total = reduce_rows(parts, dp_count, groups)
    else:
        parts = parts.reshape(groups, rows, parts.shape[1])
        moved = lax.all_to_all(parts, "expert", split_axis=0, concat_axis=0, tiled=True)
        total = lax.psum(jnp.sum(moved.astype(jnp.float32), axis=0), "dp")
    final = total[:, 2 * features : 2 * features + experts].astype(jnp.float32)
    weight_grad = jnp.sum(jnp.where(hot, final[:, None, :], 0.0), axis=2)
    return (
        total[:, :features].astype(jnp.bfloat16),
        total[:, features : 2 * features].astype(jnp.bfloat16),
        weight_grad,
    )


def solution(mesh):
    row = P("expert", None)
    cut = P("expert", None, "dp")
    return jax.shard_map(
        local,
        mesh=mesh,
        in_specs=(row, row, row, row, cut, cut, cut),
        out_specs=(row, row, row),
        check_vma=False,
    )
```

```python
import functools
import jax
import jax.numpy as jnp
from jax import lax
from jax.experimental import pallas as pl
from jax.experimental.pallas import tpu as pltpu
from jax.sharding import PartitionSpec as P

MESH = pl.DeviceIdType.MESH
WHOLE_BYTES = 8 << 20


def place(dp_count, z_count):
    d = lax.axis_index("dp")
    e = lax.axis_index("expert")
    z = e // 2
    c = e - 2 * z
    partner = (d, 2 * z + 1 - c)
    dp_to = [(lax.rem(d + k, dp_count), e) for k in range(dp_count)]
    dp_from = [lax.rem(d + dp_count - k, dp_count) for k in range(dp_count)]
    z_to = [lax.rem(z + j, z_count) for j in range(z_count)]
    z_from = [lax.rem(z + z_count - j, z_count) for j in range(z_count)]
    return d, z, c, partner, dp_to, dp_from, z_to, z_from


def greet(d, c, partner, dp_to, z_to):
    barrier = pltpu.get_barrier_semaphore()
    peers = [partner] + dp_to[1:] + [(d, 2 * zt + c) for zt in z_to[1:]]
    for peer in peers:
        pl.semaphore_signal(barrier, inc=1, device_id=peer, device_id_type=MESH)
    pl.semaphore_wait(barrier, len(peers))


def push(src, dst, send_sem, recv_sem, peer):
    return pltpu.make_async_remote_copy(
        src_ref=src,
        dst_ref=dst,
        send_sem=send_sem,
        recv_sem=recv_sem,
        device_id=peer,
        device_id_type=MESH,
    )


def gather_kernel(dp_count, z_count, own, out, local_sem, core_s, core_r, z_s, z_r, dp_s, dp_r):
    d, z, c, partner, dp_to, dp_from, z_to, z_from = place(dp_count, z_count)
    greet(d, c, partner, dp_to, z_to)
    sent = []
    for j in range(1, z_count):
        copy = push(own.at[d], out.at[z, c, d], z_s.at[j], z_r.at[j], (d, 2 * z_to[j] + c))
        copy.start()
        sent.append(copy)
    pair = push(own, out.at[z, c], core_s.at[0], core_r.at[0], partner)
    pair.start()
    sent.append(pair)
    keep = pltpu.make_async_copy(own, out.at[z, c], local_sem)
    keep.start()
    for j in range(1, z_count):
        zs = z_from[j]
        mine = out.at[zs, c, d]
        push(mine, mine, z_s.at[j], z_r.at[j], partner).wait_recv()
        for k in range(1, dp_count):
            copy = push(mine, mine, dp_s.at[j, k], dp_r.at[j, k], dp_to[k])
            copy.start()
            sent.append(copy)
    for j in range(1, z_count):
        zs = z_from[j]
        for k in range(1, dp_count):
            theirs = out.at[zs, c, dp_from[k]]
            push(theirs, theirs, dp_s.at[j, k], dp_r.at[j, k], partner).wait_recv()
        whole = out.at[zs, c]
        copy = push(whole, whole, core_s.at[j], core_r.at[j], partner)
        copy.start()
        sent.append(copy)
    keep.wait()
    for j in range(z_count):
        other = out.at[z_from[j], 1 - c]
        push(other, other, core_s.at[j], core_r.at[j], partner).wait_recv()
    for copy in sent:
        copy.wait_send()


def reduce_kernel(
    dp_count, z_count, parts, out, half, quarter, core_in, dp_in, z_in,
    core_s, core_r, dp_s, dp_r, z_s, z_r, end_s, end_r,
):
    d, z, c, partner, dp_to, dp_from, z_to, z_from = place(dp_count, z_count)
    greet(d, c, partner, dp_to, z_to)
    order = list(range(1, z_count)) + [0]
    sent = []
    for j in order:
        copy = push(
            parts.at[z_to[j], 1 - c], core_in.at[j], core_s.at[j], core_r.at[j], partner
        )
        copy.start()
        sent.append(copy)
    for j in order:
        push(core_in.at[j], core_in.at[j], core_s.at[j], core_r.at[j], partner).wait_recv()
        for k in list(range(1, dp_count)) + [0]:
            to = dp_to[k][0]
            half[j, k] = (
                parts[z_to[j], c, to].astype(jnp.float32) + core_in[j, to].astype(jnp.float32)
            ).astype(half.dtype)
            if k > 0:
                copy = push(
                    half.at[j, k], dp_in.at[j, k], dp_s.at[j, k], dp_r.at[j, k], dp_to[k]
                )
                copy.start()
                sent.append(copy)
    for j in order:
        total = half[j, 0].astype(jnp.float32)
        for k in range(1, dp_count):
            slot = dp_in.at[j, k]
            push(slot, slot, dp_s.at[j, k], dp_r.at[j, k], partner).wait_recv()
            total = total + dp_in[j, k].astype(jnp.float32)
        if j > 0:
            quarter[j] = total.astype(quarter.dtype)
            copy = push(
                quarter.at[j], z_in.at[j], z_s.at[j], z_r.at[j], (d, 2 * z_to[j] + c)
            )
            copy.start()
            sent.append(copy)
    for j in range(1, z_count):
        push(z_in.at[j], z_in.at[j], z_s.at[j], z_r.at[j], partner).wait_recv()
        total = total + z_in[j].astype(jnp.float32)
    out[d] = total.astype(out.dtype)
    for k in range(1, dp_count):
        copy = push(out.at[d], out.at[d], end_s.at[k], end_r.at[k], dp_to[k])
        copy.start()
        sent.append(copy)
    for k in range(1, dp_count):
        theirs = out.at[dp_from[k]]
        push(theirs, theirs, end_s.at[k], end_r.at[k], partner).wait_recv()
    for copy in sent:
        copy.wait_send()


def expert_kernel(
    features, experts, tile, me_ref, got, gate, up, down, out, mixed_sum, grad_sum, wide_sum
):
    step = pl.program_id(0)
    steps = pl.num_programs(0)
    column = me_ref[0] * steps + step
    across = (((1,), (0,)), ((), ()))
    along = (((1,), (1,)), ((), ()))

    def dot(a, b, dims):
        return lax.dot_general(a, b, dims, preferred_element_type=jnp.float32)

    @pl.when(step == 0)
    def _():
        mixed_sum[...] = jnp.zeros_like(mixed_sum)
        grad_sum[...] = jnp.zeros_like(grad_sum)
        wide_sum[...] = jnp.zeros_like(wide_sum)

    for start in range(0, got.shape[0], tile):
        rows = slice(start, start + tile)
        tokens = got[rows, :features]
        upstream = got[rows, features : 2 * features]
        table = got[rows, 2 * features :].astype(jnp.float32)
        lane = lax.broadcasted_iota(jnp.int32, table.shape, 1)
        here = (lane == column) | (lane == column + experts)
        weight = jnp.sum(jnp.where(here, table, 0.0), axis=1, keepdims=True)
        gate_act = dot(tokens, gate[0], across)
        up_act = dot(tokens, up[0], across)
        back = dot(upstream, down[0], across)
        sig = jax.nn.sigmoid(gate_act)
        silu = gate_act * sig
        hidden = silu * up_act
        score = jnp.sum(hidden * back, axis=1, keepdims=True)
        score = jnp.where(weight > 0, score, 0.0)
        wide_sum[rows, :] += jnp.where(lane == column, score, 0.0)
        weighted = (hidden * weight).astype(jnp.bfloat16)
        back = back * weight
        slope = sig + silu * (1.0 - sig)
        grad_gate = (back * up_act * slope).astype(jnp.bfloat16)
        grad_up = (back * silu).astype(jnp.bfloat16)
        mixed_sum[rows, :] += dot(weighted, down[0], along)
        grad_sum[rows, :] += dot(grad_gate, gate[0], along) + dot(grad_up, up[0], along)

    @pl.when(step == steps - 1)
    def _():
        out[:, :features] = mixed_sum[...].astype(out.dtype)
        out[:, features : 2 * features] = grad_sum[...].astype(out.dtype)
        out[:, 2 * features :] = wide_sum[...].astype(out.dtype)


def expert_rows(got, gate_weight, up_weight, down_weight, me, experts):
    count, features, hidden = gate_weight.shape
    rows, width = got.shape
    tile = 256 if rows % 256 == 0 else rows
    resident = pl.BlockSpec((rows, width), lambda i: (0, 0))
    streamed = pl.BlockSpec((1, features, hidden), lambda i: (i, 0, 0))
    return pl.pallas_call(
        functools.partial(expert_kernel, features, experts, tile),
        grid=(count,),
        out_shape=jax.ShapeDtypeStruct((rows, width), got.dtype),
        in_specs=[
            pl.BlockSpec(memory_space=pltpu.SMEM),
            resident,
            streamed,
            streamed,
            streamed,
        ],
        out_specs=resident,
        scratch_shapes=[
            pltpu.VMEM((rows, features), jnp.float32),
            pltpu.VMEM((rows, features), jnp.float32),
            pltpu.VMEM((rows, width - 2 * features), jnp.float32),
        ],
        compiler_params=pltpu.CompilerParams(vmem_limit_bytes=50 << 20),
    )(me.reshape(1).astype(jnp.int32), got, gate_weight, up_weight, down_weight)


def gather_rows(payload, dp_count, groups):
    rows, width = payload.shape
    z_count = groups // 2
    quarter = rows // dp_count
    dma = pltpu.SemaphoreType.DMA
    out = pl.pallas_call(
        functools.partial(gather_kernel, dp_count, z_count),
        out_shape=jax.ShapeDtypeStruct((z_count, 2, dp_count, quarter, width), payload.dtype),
        in_specs=[pl.BlockSpec(memory_space=pltpu.VMEM)],
        out_specs=pl.BlockSpec(memory_space=pltpu.VMEM),
        scratch_shapes=[dma]
        + [dma((z_count,))] * 4
        + [dma((z_count, dp_count))] * 2,
        compiler_params=pltpu.CompilerParams(
            collective_id=0, has_side_effects=True, vmem_limit_bytes=32 << 20
        ),
    )(payload.reshape(dp_count, quarter, width))
    return out.reshape(groups * rows, width)


def reduce_rows(parts, dp_count, groups):
    width = parts.shape[1]
    z_count = groups // 2
    quarter = parts.shape[0] // groups // dp_count
    dma = pltpu.SemaphoreType.DMA
    kind = parts.dtype
    out = pl.pallas_call(
        functools.partial(reduce_kernel, dp_count, z_count),
        out_shape=jax.ShapeDtypeStruct((dp_count, quarter, width), kind),
        in_specs=[pl.BlockSpec(memory_space=pltpu.VMEM)],
        out_specs=pl.BlockSpec(memory_space=pltpu.VMEM),
        scratch_shapes=[
            pltpu.VMEM((z_count, dp_count, quarter, width), kind),
            pltpu.VMEM((z_count, quarter, width), kind),
            pltpu.VMEM((z_count, dp_count, quarter, width), kind),
            pltpu.VMEM((z_count, dp_count, quarter, width), kind),
            pltpu.VMEM((z_count, quarter, width), kind),
        ]
        + [dma((z_count,))] * 2
        + [dma((z_count, dp_count))] * 2
        + [dma((z_count,))] * 2
        + [dma((dp_count,))] * 2,
        compiler_params=pltpu.CompilerParams(
            collective_id=1, has_side_effects=True, vmem_limit_bytes=48 << 20
        ),
    )(parts.reshape(z_count, 2, dp_count, quarter, width))
    return out.reshape(dp_count * quarter, width)


def dense_parts(got, gate_weight, up_weight, down_weight, me, experts):
    local_experts, features = gate_weight.shape[:2]
    tokens = got[:, :features]
    upstream = got[:, features : 2 * features]
    mine_high = lax.dynamic_slice_in_dim(got, 2 * features + me * local_experts, local_experts, 1)
    mine_low = lax.dynamic_slice_in_dim(
        got, 2 * features + experts + me * local_experts, local_experts, 1
    )
    weight = mine_high.astype(jnp.float32) + mine_low.astype(jnp.float32)
    weight = weight.T[:, :, None]
    gate_act = jnp.einsum("tl,elh->eth", tokens, gate_weight, preferred_element_type=jnp.float32)
    up_act = jnp.einsum("tl,elh->eth", tokens, up_weight, preferred_element_type=jnp.float32)
    back = jnp.einsum("tl,elh->eth", upstream, down_weight, preferred_element_type=jnp.float32)
    sig = jax.nn.sigmoid(gate_act)
    silu = gate_act * sig
    hidden = silu * up_act
    valid = (weight > 0).astype(jnp.float32)
    score = jnp.sum(hidden * back * valid, axis=2).T
    weighted = (hidden * weight).astype(jnp.bfloat16)
    back = back * weight
    slope = sig * (1.0 + gate_act * (1.0 - sig))
    grad_gate = (back * up_act * slope).astype(jnp.bfloat16)
    grad_up = (back * silu).astype(jnp.bfloat16)
    mixed = jnp.einsum("eth,elh->tl", weighted, down_weight, preferred_element_type=jnp.float32)
    grad = jnp.einsum("eth,elh->tl", grad_gate, gate_weight, preferred_element_type=jnp.float32)
    grad = grad + jnp.einsum("eth,elh->tl", grad_up, up_weight, preferred_element_type=jnp.float32)
    wide = jnp.zeros((got.shape[0], 2 * experts), jnp.float32)
    wide = lax.dynamic_update_slice_in_dim(wide, score, me * local_experts, 1)
    parts = jnp.concatenate([mixed, grad, wide], axis=1).astype(jnp.bfloat16)
    return parts


def local(latents, out_grad, routes, route_weights, gate_weight, up_weight, down_weight):
    features = latents.shape[1]
    local_experts = gate_weight.shape[0]
    groups = lax.axis_size("expert")
    experts = local_experts * groups
    me = lax.axis_index("expert")
    hot = routes[:, :, None] == jnp.arange(experts, dtype=jnp.int32)[None, None, :]
    table = jnp.sum(jnp.where(hot, route_weights[:, :, None], 0.0), axis=1)
    high = table.astype(jnp.bfloat16)
    low = (table - high.astype(jnp.float32)).astype(jnp.bfloat16)
    payload = jnp.concatenate([latents, out_grad, high, low], axis=1)
    dp_count = lax.axis_size("dp")
    rows = latents.shape[0]
    fits = rows % (16 * dp_count) == 0 and groups * payload.size * 2 <= WHOLE_BYTES
    if fits:
        got = gather_rows(payload, dp_count, groups)
        parts = expert_rows(got, gate_weight, up_weight, down_weight, me, experts)
        total = reduce_rows(parts, dp_count, groups)
    else:
        got = lax.all_gather(payload, "expert", axis=0, tiled=True)
        parts = dense_parts(got, gate_weight, up_weight, down_weight, me, experts)
        parts = parts.reshape(groups, rows, parts.shape[1])
        moved = lax.all_to_all(parts, "expert", split_axis=0, concat_axis=0, tiled=True)
        total = lax.psum(jnp.sum(moved.astype(jnp.float32), axis=0), "dp")
    final = total[:, 2 * features : 2 * features + experts].astype(jnp.float32)
    weight_grad = jnp.sum(jnp.where(hot, final[:, None, :], 0.0), axis=2)
    return (
        total[:, :features].astype(jnp.bfloat16),
        total[:, features : 2 * features].astype(jnp.bfloat16),
        weight_grad,
    )


def solution(mesh):
    row = P("expert", None)
    cut = P("expert", None, "dp")
    return jax.shard_map(
        local,
        mesh=mesh,
        in_specs=(row, row, row, row, cut, cut, cut),
        out_specs=(row, row, row),
        check_vma=False,
    )
```

```python
import functools
import jax
import jax.numpy as jnp
from jax import lax
from jax.experimental import pallas as pl
from jax.experimental.pallas import tpu as pltpu
from jax.sharding import PartitionSpec as P

MESH = pl.DeviceIdType.MESH
WHOLE_BYTES = 8 << 20


def place(dp_count, z_count):
    d = lax.axis_index("dp")
    e = lax.axis_index("expert")
    z = e // 2
    c = e - 2 * z
    partner = (d, 2 * z + 1 - c)
    dp_to = [(lax.rem(d + k, dp_count), e) for k in range(dp_count)]
    dp_from = [lax.rem(d + dp_count - k, dp_count) for k in range(dp_count)]
    z_to = [lax.rem(z + j, z_count) for j in range(z_count)]
    z_from = [lax.rem(z + z_count - j, z_count) for j in range(z_count)]
    return d, z, c, partner, dp_to, dp_from, z_to, z_from


def greet(d, c, partner, dp_to, z_to):
    barrier = pltpu.get_barrier_semaphore()
    peers = [partner] + dp_to[1:] + [(d, 2 * zt + c) for zt in z_to[1:]]
    for peer in peers:
        pl.semaphore_signal(barrier, inc=1, device_id=peer, device_id_type=MESH)
    pl.semaphore_wait(barrier, len(peers))


def push(src, dst, send_sem, recv_sem, peer):
    return pltpu.make_async_remote_copy(
        src_ref=src,
        dst_ref=dst,
        send_sem=send_sem,
        recv_sem=recv_sem,
        device_id=peer,
        device_id_type=MESH,
    )


def gather_kernel(dp_count, z_count, own, out, local_sem, core_s, core_r, z_s, z_r, dp_s, dp_r):
    d, z, c, partner, dp_to, dp_from, z_to, z_from = place(dp_count, z_count)
    greet(d, c, partner, dp_to, z_to)
    sent = []
    for j in range(1, z_count):
        copy = push(own.at[d], out.at[z, c, d], z_s.at[j], z_r.at[j], (d, 2 * z_to[j] + c))
        copy.start()
        sent.append(copy)
    pair = push(own, out.at[z, c], core_s.at[0], core_r.at[0], partner)
    pair.start()
    sent.append(pair)
    keep = pltpu.make_async_copy(own, out.at[z, c], local_sem)
    keep.start()
    for j in range(1, z_count):
        zs = z_from[j]
        mine = out.at[zs, c, d]
        push(mine, mine, z_s.at[j], z_r.at[j], partner).wait_recv()
        for k in range(1, dp_count):
            copy = push(mine, mine, dp_s.at[j, k], dp_r.at[j, k], dp_to[k])
            copy.start()
            sent.append(copy)
    for j in range(1, z_count):
        zs = z_from[j]
        for k in range(1, dp_count):
            theirs = out.at[zs, c, dp_from[k]]
            push(theirs, theirs, dp_s.at[j, k], dp_r.at[j, k], partner).wait_recv()
        whole = out.at[zs, c]
        copy = push(whole, whole, core_s.at[j], core_r.at[j], partner)
        copy.start()
        sent.append(copy)
    keep.wait()
    for j in range(z_count):
        other = out.at[z_from[j], 1 - c]
        push(other, other, core_s.at[j], core_r.at[j], partner).wait_recv()
    for copy in sent:
        copy.wait_send()


def reduce_kernel(
    dp_count, z_count, parts, out, half, quarter, core_in, dp_in, z_in,
    core_s, core_r, dp_s, dp_r, z_s, z_r, end_s, end_r,
):
    d, z, c, partner, dp_to, dp_from, z_to, z_from = place(dp_count, z_count)
    greet(d, c, partner, dp_to, z_to)
    order = list(range(1, z_count)) + [0]
    sent = []
    for j in order:
        copy = push(
            parts.at[z_to[j], 1 - c], core_in.at[j], core_s.at[j], core_r.at[j], partner
        )
        copy.start()
        sent.append(copy)
    for j in order:
        push(core_in.at[j], core_in.at[j], core_s.at[j], core_r.at[j], partner).wait_recv()
        for k in list(range(1, dp_count)) + [0]:
            to = dp_to[k][0]
            half[j, k] = (
                parts[z_to[j], c, to].astype(jnp.float32) + core_in[j, to].astype(jnp.float32)
            ).astype(half.dtype)
            if k > 0:
                copy = push(
                    half.at[j, k], dp_in.at[j, k], dp_s.at[j, k], dp_r.at[j, k], dp_to[k]
                )
                copy.start()
                sent.append(copy)
    for j in order:
        total = half[j, 0].astype(jnp.float32)
        for k in range(1, dp_count):
            slot = dp_in.at[j, k]
            push(slot, slot, dp_s.at[j, k], dp_r.at[j, k], partner).wait_recv()
            total = total + dp_in[j, k].astype(jnp.float32)
        if j > 0:
            quarter[j] = total.astype(quarter.dtype)
            copy = push(
                quarter.at[j], z_in.at[j], z_s.at[j], z_r.at[j], (d, 2 * z_to[j] + c)
            )
            copy.start()
            sent.append(copy)
    for j in range(1, z_count):
        push(z_in.at[j], z_in.at[j], z_s.at[j], z_r.at[j], partner).wait_recv()
        total = total + z_in[j].astype(jnp.float32)
    out[d] = total.astype(out.dtype)
    for k in range(1, dp_count):
        copy = push(out.at[d], out.at[d], end_s.at[k], end_r.at[k], dp_to[k])
        copy.start()
        sent.append(copy)
    for k in range(1, dp_count):
        theirs = out.at[dp_from[k]]
        push(theirs, theirs, end_s.at[k], end_r.at[k], partner).wait_recv()
    for copy in sent:
        copy.wait_send()


def expert_kernel(
    features, experts, tile, me_ref, got, gate, up, down, out, mixed_sum, grad_sum, wide_sum
):
    step = pl.program_id(0)
    steps = pl.num_programs(0)
    column = me_ref[0] * steps + step
    across = (((1,), (1,)), ((), ()))
    along = (((1,), (0,)), ((), ()))

    def dot(a, b, dims):
        return lax.dot_general(a, b, dims, preferred_element_type=jnp.float32)

    @pl.when(step == 0)
    def _():
        mixed_sum[...] = jnp.zeros_like(mixed_sum)
        grad_sum[...] = jnp.zeros_like(grad_sum)
        wide_sum[...] = jnp.zeros_like(wide_sum)

    for start in range(0, got.shape[0], tile):
        rows = slice(start, start + tile)
        tokens = got[rows, :features]
        upstream = got[rows, features : 2 * features]
        table = got[rows, 2 * features :].astype(jnp.float32)
        lane = lax.broadcasted_iota(jnp.int32, table.shape, 1)
        here = (lane == column) | (lane == column + experts)
        weight = jnp.sum(jnp.where(here, table, 0.0), axis=1, keepdims=True)
        gate_act = dot(tokens, gate[0], across)
        up_act = dot(tokens, up[0], across)
        back = dot(upstream, down[0], across)
        sig = jax.nn.sigmoid(gate_act)
        silu = gate_act * sig
        hidden = silu * up_act
        score = jnp.sum(hidden * back, axis=1, keepdims=True)
        score = jnp.where(weight > 0, score, 0.0)
        wide_sum[rows, :] += jnp.where(lane == column, score, 0.0)
        weighted = (hidden * weight).astype(jnp.bfloat16)
        back = back * weight
        slope = sig + silu * (1.0 - sig)
        grad_gate = (back * up_act * slope).astype(jnp.bfloat16)
        grad_up = (back * silu).astype(jnp.bfloat16)
        mixed_sum[rows, :] += dot(weighted, down[0], along)
        grad_sum[rows, :] += dot(grad_gate, gate[0], along) + dot(grad_up, up[0], along)

    @pl.when(step == steps - 1)
    def _():
        out[:, :features] = mixed_sum[...].astype(out.dtype)
        out[:, features : 2 * features] = grad_sum[...].astype(out.dtype)
        out[:, 2 * features :] = wide_sum[...].astype(out.dtype)


def expert_rows(got, gate_weight, up_weight, down_weight, me, experts):
    count, features, hidden = gate_weight.shape
    rows, width = got.shape
    tile = 256 if rows % 256 == 0 else rows
    resident = pl.BlockSpec((rows, width), lambda i: (0, 0))
    streamed = pl.BlockSpec((1, hidden, features), lambda i: (i, 0, 0))
    turned = [jnp.swapaxes(w, 1, 2) for w in (gate_weight, up_weight, down_weight)]
    return pl.pallas_call(
        functools.partial(expert_kernel, features, experts, tile),
        grid=(count,),
        out_shape=jax.ShapeDtypeStruct((rows, width), got.dtype),
        in_specs=[
            pl.BlockSpec(memory_space=pltpu.SMEM),
            resident,
            streamed,
            streamed,
            streamed,
        ],
        out_specs=resident,
        scratch_shapes=[
            pltpu.VMEM((rows, features), jnp.float32),
            pltpu.VMEM((rows, features), jnp.float32),
            pltpu.VMEM((rows, width - 2 * features), jnp.float32),
        ],
        compiler_params=pltpu.CompilerParams(vmem_limit_bytes=50 << 20),
    )(me.reshape(1).astype(jnp.int32), got, *turned)


def gather_rows(payload, dp_count, groups):
    rows, width = payload.shape
    z_count = groups // 2
    quarter = rows // dp_count
    dma = pltpu.SemaphoreType.DMA
    out = pl.pallas_call(
        functools.partial(gather_kernel, dp_count, z_count),
        out_shape=jax.ShapeDtypeStruct((z_count, 2, dp_count, quarter, width), payload.dtype),
        in_specs=[pl.BlockSpec(memory_space=pltpu.VMEM)],
        out_specs=pl.BlockSpec(memory_space=pltpu.VMEM),
        scratch_shapes=[dma]
        + [dma((z_count,))] * 4
        + [dma((z_count, dp_count))] * 2,
        compiler_params=pltpu.CompilerParams(
            collective_id=0, has_side_effects=True, vmem_limit_bytes=32 << 20
        ),
    )(payload.reshape(dp_count, quarter, width))
    return out.reshape(groups * rows, width)


def reduce_rows(parts, dp_count, groups):
    width = parts.shape[1]
    z_count = groups // 2
    quarter = parts.shape[0] // groups // dp_count
    dma = pltpu.SemaphoreType.DMA
    kind = parts.dtype
    out = pl.pallas_call(
        functools.partial(reduce_kernel, dp_count, z_count),
        out_shape=jax.ShapeDtypeStruct((dp_count, quarter, width), kind),
        in_specs=[pl.BlockSpec(memory_space=pltpu.VMEM)],
        out_specs=pl.BlockSpec(memory_space=pltpu.VMEM),
        scratch_shapes=[
            pltpu.VMEM((z_count, dp_count, quarter, width), kind),
            pltpu.VMEM((z_count, quarter, width), kind),
            pltpu.VMEM((z_count, dp_count, quarter, width), kind),
            pltpu.VMEM((z_count, dp_count, quarter, width), kind),
            pltpu.VMEM((z_count, quarter, width), kind),
        ]
        + [dma((z_count,))] * 2
        + [dma((z_count, dp_count))] * 2
        + [dma((z_count,))] * 2
        + [dma((dp_count,))] * 2,
        compiler_params=pltpu.CompilerParams(
            collective_id=1, has_side_effects=True, vmem_limit_bytes=48 << 20
        ),
    )(parts.reshape(z_count, 2, dp_count, quarter, width))
    return out.reshape(dp_count * quarter, width)


def dense_parts(got, gate_weight, up_weight, down_weight, me, experts):
    local_experts, features = gate_weight.shape[:2]
    tokens = got[:, :features]
    upstream = got[:, features : 2 * features]
    mine_high = lax.dynamic_slice_in_dim(got, 2 * features + me * local_experts, local_experts, 1)
    mine_low = lax.dynamic_slice_in_dim(
        got, 2 * features + experts + me * local_experts, local_experts, 1
    )
    weight = mine_high.astype(jnp.float32) + mine_low.astype(jnp.float32)
    weight = weight.T[:, :, None]
    gate_act = jnp.einsum("tl,elh->eth", tokens, gate_weight, preferred_element_type=jnp.float32)
    up_act = jnp.einsum("tl,elh->eth", tokens, up_weight, preferred_element_type=jnp.float32)
    back = jnp.einsum("tl,elh->eth", upstream, down_weight, preferred_element_type=jnp.float32)
    sig = jax.nn.sigmoid(gate_act)
    silu = gate_act * sig
    hidden = silu * up_act
    valid = (weight > 0).astype(jnp.float32)
    score = jnp.sum(hidden * back * valid, axis=2).T
    weighted = (hidden * weight).astype(jnp.bfloat16)
    back = back * weight
    slope = sig * (1.0 + gate_act * (1.0 - sig))
    grad_gate = (back * up_act * slope).astype(jnp.bfloat16)
    grad_up = (back * silu).astype(jnp.bfloat16)
    mixed = jnp.einsum("eth,elh->tl", weighted, down_weight, preferred_element_type=jnp.float32)
    grad = jnp.einsum("eth,elh->tl", grad_gate, gate_weight, preferred_element_type=jnp.float32)
    grad = grad + jnp.einsum("eth,elh->tl", grad_up, up_weight, preferred_element_type=jnp.float32)
    wide = jnp.zeros((got.shape[0], 2 * experts), jnp.float32)
    wide = lax.dynamic_update_slice_in_dim(wide, score, me * local_experts, 1)
    parts = jnp.concatenate([mixed, grad, wide], axis=1).astype(jnp.bfloat16)
    return parts


def local(latents, out_grad, routes, route_weights, gate_weight, up_weight, down_weight):
    features = latents.shape[1]
    local_experts = gate_weight.shape[0]
    groups = lax.axis_size("expert")
    experts = local_experts * groups
    me = lax.axis_index("expert")
    hot = routes[:, :, None] == jnp.arange(experts, dtype=jnp.int32)[None, None, :]
    table = jnp.sum(jnp.where(hot, route_weights[:, :, None], 0.0), axis=1)
    high = table.astype(jnp.bfloat16)
    low = (table - high.astype(jnp.float32)).astype(jnp.bfloat16)
    payload = jnp.concatenate([latents, out_grad, high, low], axis=1)
    dp_count = lax.axis_size("dp")
    rows = latents.shape[0]
    fits = rows % (16 * dp_count) == 0 and groups * payload.size * 2 <= WHOLE_BYTES
    if fits:
        got = gather_rows(payload, dp_count, groups)
        parts = expert_rows(got, gate_weight, up_weight, down_weight, me, experts)
        total = reduce_rows(parts, dp_count, groups)
    else:
        got = lax.all_gather(payload, "expert", axis=0, tiled=True)
        parts = dense_parts(got, gate_weight, up_weight, down_weight, me, experts)
        parts = parts.reshape(groups, rows, parts.shape[1])
        moved = lax.all_to_all(parts, "expert", split_axis=0, concat_axis=0, tiled=True)
        total = lax.psum(jnp.sum(moved.astype(jnp.float32), axis=0), "dp")
    final = total[:, 2 * features : 2 * features + experts].astype(jnp.float32)
    weight_grad = jnp.sum(jnp.where(hot, final[:, None, :], 0.0), axis=2)
    return (
        total[:, :features].astype(jnp.bfloat16),
        total[:, features : 2 * features].astype(jnp.bfloat16),
        weight_grad,
    )


def solution(mesh):
    row = P("expert", None)
    cut = P("expert", None, "dp")
    return jax.shard_map(
        local,
        mesh=mesh,
        in_specs=(row, row, row, row, cut, cut, cut),
        out_specs=(row, row, row),
        check_vma=False,
    )
```

```python
import functools
import jax
import jax.numpy as jnp
from jax import lax
from jax.experimental import pallas as pl
from jax.experimental.pallas import tpu as pltpu
from jax.sharding import PartitionSpec as P

MESH = pl.DeviceIdType.MESH
WHOLE_BYTES = 8 << 20


def place(dp_count, z_count):
    d = lax.axis_index("dp")
    e = lax.axis_index("expert")
    z = e // 2
    c = e - 2 * z
    partner = (d, 2 * z + 1 - c)
    dp_to = [(lax.rem(d + k, dp_count), e) for k in range(dp_count)]
    dp_from = [lax.rem(d + dp_count - k, dp_count) for k in range(dp_count)]
    z_to = [lax.rem(z + j, z_count) for j in range(z_count)]
    z_from = [lax.rem(z + z_count - j, z_count) for j in range(z_count)]
    return d, z, c, partner, dp_to, dp_from, z_to, z_from


def greet(d, c, partner, dp_to, z_to):
    barrier = pltpu.get_barrier_semaphore()
    peers = [partner] + dp_to[1:] + [(d, 2 * zt + c) for zt in z_to[1:]]
    for peer in peers:
        pl.semaphore_signal(barrier, inc=1, device_id=peer, device_id_type=MESH)
    pl.semaphore_wait(barrier, len(peers))


def push(src, dst, send_sem, recv_sem, peer):
    return pltpu.make_async_remote_copy(
        src_ref=src,
        dst_ref=dst,
        send_sem=send_sem,
        recv_sem=recv_sem,
        device_id=peer,
        device_id_type=MESH,
    )


def gather_kernel(dp_count, z_count, own, out, local_sem, core_s, core_r, z_s, z_r, dp_s, dp_r):
    d, z, c, partner, dp_to, dp_from, z_to, z_from = place(dp_count, z_count)
    greet(d, c, partner, dp_to, z_to)
    sent = []
    for j in range(1, z_count):
        copy = push(own.at[d], out.at[z, c, d], z_s.at[j], z_r.at[j], (d, 2 * z_to[j] + c))
        copy.start()
        sent.append(copy)
    pair = push(own, out.at[z, c], core_s.at[0], core_r.at[0], partner)
    pair.start()
    sent.append(pair)
    keep = pltpu.make_async_copy(own, out.at[z, c], local_sem)
    keep.start()
    for j in range(1, z_count):
        zs = z_from[j]
        mine = out.at[zs, c, d]
        push(mine, mine, z_s.at[j], z_r.at[j], partner).wait_recv()
        for k in range(1, dp_count):
            copy = push(mine, mine, dp_s.at[j, k], dp_r.at[j, k], dp_to[k])
            copy.start()
            sent.append(copy)
    for j in range(1, z_count):
        zs = z_from[j]
        for k in range(1, dp_count):
            theirs = out.at[zs, c, dp_from[k]]
            push(theirs, theirs, dp_s.at[j, k], dp_r.at[j, k], partner).wait_recv()
        whole = out.at[zs, c]
        copy = push(whole, whole, core_s.at[j], core_r.at[j], partner)
        copy.start()
        sent.append(copy)
    keep.wait()
    for j in range(z_count):
        other = out.at[z_from[j], 1 - c]
        push(other, other, core_s.at[j], core_r.at[j], partner).wait_recv()
    for copy in sent:
        copy.wait_send()


def reduce_kernel(
    dp_count, z_count, parts, out, half, quarter, core_in, dp_in, z_in,
    core_s, core_r, dp_s, dp_r, z_s, z_r, end_s, end_r,
):
    d, z, c, partner, dp_to, dp_from, z_to, z_from = place(dp_count, z_count)
    greet(d, c, partner, dp_to, z_to)
    order = list(range(1, z_count)) + [0]
    sent = []
    for j in order:
        copy = push(
            parts.at[z_to[j], 1 - c], core_in.at[j], core_s.at[j], core_r.at[j], partner
        )
        copy.start()
        sent.append(copy)
    for j in order:
        push(core_in.at[j], core_in.at[j], core_s.at[j], core_r.at[j], partner).wait_recv()
        for k in list(range(1, dp_count)) + [0]:
            to = dp_to[k][0]
            half[j, k] = (
                parts[z_to[j], c, to].astype(jnp.float32) + core_in[j, to].astype(jnp.float32)
            ).astype(half.dtype)
            if k > 0:
                copy = push(
                    half.at[j, k], dp_in.at[j, k], dp_s.at[j, k], dp_r.at[j, k], dp_to[k]
                )
                copy.start()
                sent.append(copy)
    for j in order:
        total = half[j, 0].astype(jnp.float32)
        for k in range(1, dp_count):
            slot = dp_in.at[j, k]
            push(slot, slot, dp_s.at[j, k], dp_r.at[j, k], partner).wait_recv()
            total = total + dp_in[j, k].astype(jnp.float32)
        if j > 0:
            quarter[j] = total.astype(quarter.dtype)
            copy = push(
                quarter.at[j], z_in.at[j], z_s.at[j], z_r.at[j], (d, 2 * z_to[j] + c)
            )
            copy.start()
            sent.append(copy)
    for j in range(1, z_count):
        push(z_in.at[j], z_in.at[j], z_s.at[j], z_r.at[j], partner).wait_recv()
        total = total + z_in[j].astype(jnp.float32)
    out[d] = total.astype(out.dtype)
    for k in range(1, dp_count):
        copy = push(out.at[d], out.at[d], end_s.at[k], end_r.at[k], dp_to[k])
        copy.start()
        sent.append(copy)
    for k in range(1, dp_count):
        theirs = out.at[dp_from[k]]
        push(theirs, theirs, end_s.at[k], end_r.at[k], partner).wait_recv()
    for copy in sent:
        copy.wait_send()


def expert_kernel(
    features, experts, tile, me_ref, got, gate, up, down, out, mixed_sum, grad_sum, wide_sum
):
    step = pl.program_id(0)
    steps = pl.num_programs(0)
    column = me_ref[0] * steps + step
    across = (((1,), (1,)), ((), ()))
    along = (((1,), (0,)), ((), ()))

    def dot(a, b, dims):
        return lax.dot_general(a, b, dims, preferred_element_type=jnp.float32)

    @pl.when(step == 0)
    def _():
        mixed_sum[...] = jnp.zeros_like(mixed_sum)
        grad_sum[...] = jnp.zeros_like(grad_sum)
        wide_sum[...] = jnp.zeros_like(wide_sum)

    for start in range(0, got.shape[0], tile):
        rows = slice(start, start + tile)
        tokens = got[rows, :features]
        upstream = got[rows, features : 2 * features]
        table = got[rows, 2 * features :].astype(jnp.float32)
        lane = lax.broadcasted_iota(jnp.int32, table.shape, 1)
        here = (lane == column) | (lane == column + experts)
        weight = jnp.sum(jnp.where(here, table, 0.0), axis=1, keepdims=True)
        gate_act = dot(tokens, gate[0], across)
        up_act = dot(tokens, up[0], across)
        back = dot(upstream, down[0], across)
        sig = jax.nn.sigmoid(gate_act)
        silu = gate_act * sig
        hidden = silu * up_act
        score = jnp.sum(hidden * back, axis=1, keepdims=True)
        score = jnp.where(weight > 0, score, 0.0)
        wide_sum[rows, :] += jnp.where(lane == column, score, 0.0)
        weighted = (hidden * weight).astype(jnp.bfloat16)
        back = back * weight
        slope = sig + silu * (1.0 - sig)
        grad_gate = (back * up_act * slope).astype(jnp.bfloat16)
        grad_up = (back * silu).astype(jnp.bfloat16)
        mixed_sum[rows, :] += dot(weighted, down[0], along)
        grad_sum[rows, :] += dot(grad_gate, gate[0], along) + dot(grad_up, up[0], along)

    @pl.when(step == steps - 1)
    def _():
        out[:, :features] = mixed_sum[...].astype(out.dtype)
        out[:, features : 2 * features] = grad_sum[...].astype(out.dtype)
        out[:, 2 * features :] = wide_sum[...].astype(out.dtype)


def expert_rows(got, gate_weight, up_weight, down_weight, me, experts):
    count, features, hidden = gate_weight.shape
    rows, width = got.shape
    tile = 512 if rows % 512 == 0 else rows
    resident = pl.BlockSpec((rows, width), lambda i: (0, 0))
    streamed = pl.BlockSpec((1, hidden, features), lambda i: (i, 0, 0))
    turned = [jnp.swapaxes(w, 1, 2) for w in (gate_weight, up_weight, down_weight)]
    return pl.pallas_call(
        functools.partial(expert_kernel, features, experts, tile),
        grid=(count,),
        out_shape=jax.ShapeDtypeStruct((rows, width), got.dtype),
        in_specs=[
            pl.BlockSpec(memory_space=pltpu.SMEM),
            resident,
            streamed,
            streamed,
            streamed,
        ],
        out_specs=resident,
        scratch_shapes=[
            pltpu.VMEM((rows, features), jnp.float32),
            pltpu.VMEM((rows, features), jnp.float32),
            pltpu.VMEM((rows, width - 2 * features), jnp.float32),
        ],
        compiler_params=pltpu.CompilerParams(vmem_limit_bytes=50 << 20),
    )(me.reshape(1).astype(jnp.int32), got, *turned)


def gather_rows(payload, dp_count, groups):
    rows, width = payload.shape
    z_count = groups // 2
    quarter = rows // dp_count
    dma = pltpu.SemaphoreType.DMA
    out = pl.pallas_call(
        functools.partial(gather_kernel, dp_count, z_count),
        out_shape=jax.ShapeDtypeStruct((z_count, 2, dp_count, quarter, width), payload.dtype),
        in_specs=[pl.BlockSpec(memory_space=pltpu.VMEM)],
        out_specs=pl.BlockSpec(memory_space=pltpu.VMEM),
        scratch_shapes=[dma]
        + [dma((z_count,))] * 4
        + [dma((z_count, dp_count))] * 2,
        compiler_params=pltpu.CompilerParams(
            collective_id=0, has_side_effects=True, vmem_limit_bytes=32 << 20
        ),
    )(payload.reshape(dp_count, quarter, width))
    return out.reshape(groups * rows, width)


def reduce_rows(parts, dp_count, groups):
    width = parts.shape[1]
    z_count = groups // 2
    quarter = parts.shape[0] // groups // dp_count
    dma = pltpu.SemaphoreType.DMA
    kind = parts.dtype
    out = pl.pallas_call(
        functools.partial(reduce_kernel, dp_count, z_count),
        out_shape=jax.ShapeDtypeStruct((dp_count, quarter, width), kind),
        in_specs=[pl.BlockSpec(memory_space=pltpu.VMEM)],
        out_specs=pl.BlockSpec(memory_space=pltpu.VMEM),
        scratch_shapes=[
            pltpu.VMEM((z_count, dp_count, quarter, width), kind),
            pltpu.VMEM((z_count, quarter, width), kind),
            pltpu.VMEM((z_count, dp_count, quarter, width), kind),
            pltpu.VMEM((z_count, dp_count, quarter, width), kind),
            pltpu.VMEM((z_count, quarter, width), kind),
        ]
        + [dma((z_count,))] * 2
        + [dma((z_count, dp_count))] * 2
        + [dma((z_count,))] * 2
        + [dma((dp_count,))] * 2,
        compiler_params=pltpu.CompilerParams(
            collective_id=1, has_side_effects=True, vmem_limit_bytes=48 << 20
        ),
    )(parts.reshape(z_count, 2, dp_count, quarter, width))
    return out.reshape(dp_count * quarter, width)


def dense_parts(got, gate_weight, up_weight, down_weight, me, experts):
    local_experts, features = gate_weight.shape[:2]
    tokens = got[:, :features]
    upstream = got[:, features : 2 * features]
    mine_high = lax.dynamic_slice_in_dim(got, 2 * features + me * local_experts, local_experts, 1)
    mine_low = lax.dynamic_slice_in_dim(
        got, 2 * features + experts + me * local_experts, local_experts, 1
    )
    weight = mine_high.astype(jnp.float32) + mine_low.astype(jnp.float32)
    weight = weight.T[:, :, None]
    gate_act = jnp.einsum("tl,elh->eth", tokens, gate_weight, preferred_element_type=jnp.float32)
    up_act = jnp.einsum("tl,elh->eth", tokens, up_weight, preferred_element_type=jnp.float32)
    back = jnp.einsum("tl,elh->eth", upstream, down_weight, preferred_element_type=jnp.float32)
    sig = jax.nn.sigmoid(gate_act)
    silu = gate_act * sig
    hidden = silu * up_act
    valid = (weight > 0).astype(jnp.float32)
    score = jnp.sum(hidden * back * valid, axis=2).T
    weighted = (hidden * weight).astype(jnp.bfloat16)
    back = back * weight
    slope = sig * (1.0 + gate_act * (1.0 - sig))
    grad_gate = (back * up_act * slope).astype(jnp.bfloat16)
    grad_up = (back * silu).astype(jnp.bfloat16)
    mixed = jnp.einsum("eth,elh->tl", weighted, down_weight, preferred_element_type=jnp.float32)
    grad = jnp.einsum("eth,elh->tl", grad_gate, gate_weight, preferred_element_type=jnp.float32)
    grad = grad + jnp.einsum("eth,elh->tl", grad_up, up_weight, preferred_element_type=jnp.float32)
    wide = jnp.zeros((got.shape[0], 2 * experts), jnp.float32)
    wide = lax.dynamic_update_slice_in_dim(wide, score, me * local_experts, 1)
    parts = jnp.concatenate([mixed, grad, wide], axis=1).astype(jnp.bfloat16)
    return parts


def local(latents, out_grad, routes, route_weights, gate_weight, up_weight, down_weight):
    features = latents.shape[1]
    local_experts = gate_weight.shape[0]
    groups = lax.axis_size("expert")
    experts = local_experts * groups
    me = lax.axis_index("expert")
    hot = routes[:, :, None] == jnp.arange(experts, dtype=jnp.int32)[None, None, :]
    table = jnp.sum(jnp.where(hot, route_weights[:, :, None], 0.0), axis=1)
    high = table.astype(jnp.bfloat16)
    low = (table - high.astype(jnp.float32)).astype(jnp.bfloat16)
    payload = jnp.concatenate([latents, out_grad, high, low], axis=1)
    dp_count = lax.axis_size("dp")
    rows = latents.shape[0]
    fits = rows % (16 * dp_count) == 0 and groups * payload.size * 2 <= WHOLE_BYTES
    if fits:
        got = gather_rows(payload, dp_count, groups)
        parts = expert_rows(got, gate_weight, up_weight, down_weight, me, experts)
        total = reduce_rows(parts, dp_count, groups)
    else:
        got = lax.all_gather(payload, "expert", axis=0, tiled=True)
        parts = dense_parts(got, gate_weight, up_weight, down_weight, me, experts)
        parts = parts.reshape(groups, rows, parts.shape[1])
        moved = lax.all_to_all(parts, "expert", split_axis=0, concat_axis=0, tiled=True)
        total = lax.psum(jnp.sum(moved.astype(jnp.float32), axis=0), "dp")
    final = total[:, 2 * features : 2 * features + experts].astype(jnp.float32)
    weight_grad = jnp.sum(jnp.where(hot, final[:, None, :], 0.0), axis=2)
    return (
        total[:, :features].astype(jnp.bfloat16),
        total[:, features : 2 * features].astype(jnp.bfloat16),
        weight_grad,
    )


def solution(mesh):
    row = P("expert", None)
    cut = P("expert", None, "dp")
    return jax.shard_map(
        local,
        mesh=mesh,
        in_specs=(row, row, row, row, cut, cut, cut),
        out_specs=(row, row, row),
        check_vma=False,
    )
```
